512 devices in a mesh: gx: 16 (over z), gy: 32 (over y, x, core).
Axes of the slice: x: 4, y: 4, z: 16, core: 2. Of those that a mesh axis runs over, the one named last changes fastest.
Arguments:
- field_now: float32 [512, 8, 4096], P('gx', None, 'gy'), may hold values from -6 to 6
- base_cond: float32 [512, 8, 4096], P('gx', None, 'gy'), may hold values from 1.4 to 2.8
- spacing: float32 [512], P('gx'), may hold values from 0.45 to 0.65
- source: float32 [512, 8, 4096], P('gx', None, 'gy'), may hold values from -6 to 7.5
Outputs:
- field_half: float32 [512, 8, 4096], P('gx', None, 'gy')
- face_flux: float32 [512, 8, 4096], P('gx', None, 'gy')
The draws below stay inside these ranges and needn't reach their ends.
All inputs are finite; a program needn't handle non-finite values.
Results may differ from the reference program's by a relative error of at most 0.0019.
Values sent between devices are 32-bit elements; how exact they have to be, the bound alone decides.
A program may use at most 64 MiB of HBM per device.

```python
import math
import jax
import jax.numpy as jnp
from jax import lax

CX = 32
NZ = 8
STIFF = 4096
NX = 512
NY = 4096


def draw_source(key, part):
    key = jax.random.fold_in(key, 11)
    noise_key, shift_key, level_key = jax.random.split(key, 3)
    cells = jnp.arange(NX, dtype=jnp.int32)
    offset_cells = jax.random.randint(shift_key, (), 0, NX, dtype=jnp.int32)
    block = (cells * 4 + offset_cells) // NX
    levels = jax.random.uniform(level_key, (5,), jnp.float32, -2.5, 2.5)
    labels = jnp.arange(5, dtype=jnp.int32)
    profile = jnp.sum(jnp.where(block[:, None] == labels[None, :], levels[None, :], 0.0), axis=1)
    noise = 0.8 * jnp.clip(jax.random.normal(noise_key, (NX, NZ, NY), jnp.float32), -3.0, 3.0)
    base_level = 1.0
    return noise + base_level + profile[:, None, None]


def block_levels(own_key, extent, shards, smallest, largest):
    loudness = 1.0
    for dim, parts in shards:
        heights = jax.random.uniform(jax.random.fold_in(jax.random.fold_in(own_key, 6), dim), (parts,), jnp.float32, smallest / len(shards), largest / len(shards))
        loudness = loudness * jnp.repeat(jnp.exp(heights), extent[dim] // parts).reshape((-1,) + (1,) * (len(extent) - 1 - dim))
    return loudness


def gaussian(own_key, extent, deviation, bound, cuts=(), kind=jnp.bfloat16):
    values = deviation * jax.random.normal(own_key, extent, jnp.float32)
    if cuts:
        values = values * block_levels(own_key, extent, cuts, -0.22, 0.18)
    return jnp.clip(values, -bound, bound).astype(kind)


def setup_inputs(seed: int = 0) -> dict:
    key_list = jax.random.split(jax.random.key(seed), 5)
    field_now = gaussian(key_list[0], (NX, NZ, NY), 1.0, 6.0, ((0, 16), (2, 32)), jnp.float32)
    base_cond = jnp.clip(jnp.exp(math.log(2.8) - 0.6931472 * jax.random.uniform(key_list[1], (NX, NZ, NY), jnp.float32) ** block_levels(key_list[1], (NX, NZ, NY), ((0, 16), (2, 32)), -0.2, 0.2)), 1.4, 2.8)
    spacing = jnp.clip(jnp.exp(math.log(0.65) - 0.36772477 * jax.random.uniform(key_list[2], (NX,), jnp.float32) ** block_levels(key_list[2], (NX,), ((0, 16),), -0.2, 0.2)), 0.45, 0.65)
    source = draw_source(jax.random.fold_in(key_list[4], 71), 0)
    return {"field_now": field_now, "base_cond": base_cond, "spacing": spacing, "source": source}


y_weight = 0.15
z_weight = 0.1
source_gain = 1.0


def conduct(field, base_cond):
    square = field * field
    return base_cond * (1.0 + square / (1.0 + square))


def harmonic(first, second):
    return 2.0 * first * second / (first + second)


def x_coeffs(cond, spacing):
    cell = jnp.broadcast_to(spacing[:, None, None], cond.shape)
    cond_next = jnp.concatenate([cond[1:], cond[-1:]], 0)
    cell_next = jnp.concatenate([cell[1:], cell[-1:]], 0)
    cond_prev = jnp.concatenate([cond[:1], cond[:-1]], 0)
    cell_prev = jnp.concatenate([cell[:1], cell[:-1]], 0)
    w_up = STIFF * harmonic(cond, cond_next) / (0.5 * (cell + cell_next))
    w_down = STIFF * harmonic(cond, cond_prev) / (0.5 * (cell + cell_prev))
    return cell, w_up, w_down


def thomas(sub_diag, main_diag, sup_diag, right):
    sub_diag = sub_diag.at[0].set(0.0)
    start = jnp.zeros(right.shape[1:], right.dtype)

    def forward(carry, row):
        ratio_prev, value_prev = carry
        lower, middle, upper, known = row
        denom = middle - lower * ratio_prev
        ratio = upper / denom
        value = (known - lower * value_prev) / denom
        return (ratio, value), (ratio, value)

    _, (ratios, values) = lax.scan(forward, (start, start), (sub_diag, main_diag, sup_diag, right))

    def backward(after, row):
        ratio, value = row
        result = value - ratio * after
        return result, result

    _, solved = lax.scan(backward, start, (ratios, values), reverse=True)
    return solved


def implicit_solve(cond, spacing, right):
    cell, w_up, w_down = x_coeffs(cond, spacing)
    return thomas(-w_down, cell + w_up + w_down, -w_up, right), w_up


def reference(field_now, base_cond, spacing, source):
    cond_start = conduct(field_now, base_cond)
    pad_field = jnp.pad(field_now, ((0, 0), (0, 0), (1, 1)))
    pad_cond = jnp.pad(cond_start, ((0, 0), (0, 0), (1, 1)))
    dy = y_weight * harmonic(cond_start, pad_cond[:, :, 2:]) * (pad_field[:, :, 2:] - field_now)
    dy = dy + y_weight * harmonic(cond_start, pad_cond[:, :, :-2]) * (pad_field[:, :, :-2] - field_now)
    face_z = z_weight * harmonic(cond_start[:, :-1], cond_start[:, 1:]) * (field_now[:, 1:] - field_now[:, :-1])
    zero_face = jnp.zeros_like(face_z[:, :1])
    dz = jnp.concatenate([face_z, zero_face], 1) - jnp.concatenate([zero_face, face_z], 1)
    cell = spacing[:, None, None]
    right = cell * (field_now + dy + dz + source_gain * source)
    field_first, _ = implicit_solve(cond_start, spacing, right)
    cond_next = conduct(0.5 * (field_now + field_first), base_cond)
    field_half, w_up = implicit_solve(cond_next, spacing, right)
    ahead = jnp.concatenate([field_half[1:], jnp.zeros_like(field_half[:1])], 0)
    face_flux = w_up * (field_half - ahead) / CX
    return field_half, face_flux
```

```python
import functools

import jax
import jax.numpy as jnp
from jax import lax
from jax.experimental import pallas as pl
from jax.experimental.pallas import tpu as pltpu
from jax.sharding import PartitionSpec as P

MESH = pl.DeviceIdType.MESH
CELLS = 32
COEFS = 6
FIRST_ROOT = 5
SECOND_ROOT = 0


def resistivity(field, base_cond):
    square = field * field
    return (1.0 + square) / (base_cond * (1.0 + 2.0 * square))


def kernel(
    parts,
    rows,
    h_ref,
    f_ref,
    k_ref,
    s_ref,
    u_out,
    flux_out,
    q_ref,
    r_ref,
    rho_ref,
    edge,
    edge_in,
    head,
    head_in,
    coef,
    gather,
    state_out,
    state,
    y_send,
    y_recv,
    x_send,
    x_recv,
    c_send,
    c_recv,
    s_send,
    s_recv,
):
    gx = lax.axis_index("gx")
    gy = lax.axis_index("gy")
    first_root = FIRST_ROOT % parts
    second_root = SECOND_ROOT % parts
    roots = (first_root, second_root)
    next_y = lax.rem(gy + 1, rows)
    prev_y = lax.rem(gy + rows - 1, rows)
    has_up = gx < parts - 1
    has_down = gx > 0

    barrier = pltpu.get_barrier_semaphore()

    def greet(target):
        pl.semaphore_signal(barrier, inc=1, device_id=target, device_id_type=MESH)

    greet({"gy": next_y})
    greet({"gy": prev_y})

    @pl.when(has_up)
    def _():
        greet({"gx": gx + 1})

    @pl.when(has_down)
    def _():
        greet({"gx": gx - 1})

    for root in roots:

        @pl.when(gx == root)
        def _():
            for step in range(1, parts):
                greet({"gx": lax.rem(gx + step, parts)})

    greetings = 2 + has_up.astype(jnp.int32) + has_down.astype(jnp.int32)
    for root in roots:
        greetings = greetings + (gx != root).astype(jnp.int32)

    lane = lax.broadcasted_iota(jnp.int32, (8, 128), 1)
    plane = lax.broadcasted_iota(jnp.int32, (8, 128), 0)
    even = lane % 2 == 0
    pair = lane // 2

    packed = jnp.zeros((8, 128), jnp.float32)
    for i in range(CELLS):
        field = f_ref[i]
        q = resistivity(field, k_ref[i])
        q_ref[i] = q
        packed = jnp.where(pair == i, pltpu.roll(field, 2 * i + 1, 1), packed)
        packed = jnp.where(pair == i + 32, pltpu.roll(q, (64 + 2 * i + 1) % 128, 1), packed)
    edge[...] = packed
    head[0] = f_ref[0]
    head[1] = k_ref[0]
    head[2] = jnp.full((8, 128), h_ref[0], jnp.float32)

    pl.semaphore_wait(barrier, greetings)

    def y_copy(slot, target):
        return pltpu.make_async_remote_copy(
            src_ref=edge,
            dst_ref=edge_in.at[slot],
            send_sem=y_send.at[slot],
            recv_sem=y_recv.at[slot],
            device_id={"gy": target},
            device_id_type=MESH,
        )

    to_next = y_copy(0, next_y)
    to_prev = y_copy(1, prev_y)
    to_next.start()
    to_prev.start()
    to_down = pltpu.make_async_remote_copy(
        src_ref=head,
        dst_ref=head_in,
        send_sem=x_send,
        recv_sem=x_recv,
        device_id={"gx": lax.rem(gx + parts - 1, parts)},
        device_id_type=MESH,
    )

    @pl.when(has_down)
    def _():
        to_down.start()

    for i in range(CELLS):
        field, q = f_ref[i], q_ref[i]
        face_y = 0.3 / (q + pltpu.roll(q, 127, 1)) * (pltpu.roll(field, 127, 1) - field)
        face_y = jnp.where(lane == 127, 0.0, face_y)
        face_z = 0.2 / (q + pltpu.roll(q, 7, 0)) * (pltpu.roll(field, 7, 0) - field)
        face_z = jnp.where(plane == 7, 0.0, face_z)
        r_ref[i] = (
            field
            + (face_y - pltpu.roll(face_y, 1, 1))
            + (face_z - pltpu.roll(face_z, 1, 0))
            + s_ref[i]
        )

    h = [h_ref[i] for i in range(CELLS)]
    is_first = gx == 0
    is_last = gx == parts - 1

    def face_weights(q_next, h_next):
        scale = 1.0 / (16.0 * CELLS * CELLS)
        for i in range(CELLS - 1):
            rho_ref[i] = ((h[i] + h[i + 1]) * scale) * (q_ref[i] + q_ref[i + 1])
        q_last = q_ref[CELLS - 1]
        q_next = jnp.where(is_last, q_last, q_next)
        h_next = jnp.where(is_last, h[CELLS - 1], h_next)
        rho_ref[CELLS - 1] = ((h[CELLS - 1] + h_next) * scale) * (q_last + q_next)
        return jnp.where(is_first, (4.0 * h[0] * scale) * q_ref[0], 0.0)

    def transfer(rho_start, slot):
        one = jnp.ones((8, 128), jnp.float32)
        zero = jnp.zeros((8, 128), jnp.float32)
        u_a, f_a = one, zero
        u_b, f_b = zero - rho_start, one
        u_c, f_c = zero, zero
        for i in range(CELLS):
            rho = rho_ref[i]
            f_a = f_a - h[i] * u_a
            f_b = f_b - h[i] * u_b
            f_c = f_c + (r_ref[i] - h[i] * u_c)
            u_a = u_a - rho * f_a
            u_b = u_b - rho * f_b
            u_c = u_c - rho * f_c
        for c, value in enumerate((u_a, u_b, f_a, f_b, u_c, f_c)):
            coef[slot, c] = value

    def solve(root, slot):
        here = gx == root
        to_root = pltpu.make_async_remote_copy(
            src_ref=coef.at[slot],
            dst_ref=gather.at[slot, gx],
            send_sem=c_send.at[slot],
            recv_sem=c_recv.at[slot],
            device_id={"gx": root},
            device_id_type=MESH,
        )

        @pl.when(jnp.logical_not(here))
        def _():
            to_root.start()

        @pl.when(here)
        def _():
            gather[slot, root] = coef[slot]
            arrived = gather.at[slot, pl.ds(0, parts - 1)]
            pltpu.make_async_copy(arrived, arrived, c_recv.at[slot]).wait()
            zero = jnp.zeros((8, 128), jnp.float32)
            w_u, w_f = zero, zero + 1.0
            p_u, p_f = zero, zero
            entries = []
            for part in range(parts):
                entries.append((w_u, w_f, p_u, p_f))
                m11, m12, m21, m22, b_u, b_f = (gather[slot, part, c] for c in range(COEFS))
                w_u, w_f = m11 * w_u + m12 * w_f, m21 * w_u + m22 * w_f
                p_u, p_f = m11 * p_u + m12 * p_f + b_u, m21 * p_u + m22 * p_f + b_f
            start = -p_u / w_u
            for part, (w_u, w_f, p_u, p_f) in enumerate(entries):
                state_out[slot, part, 0] = w_u * start + p_u
                state_out[slot, part, 1] = w_f * start + p_f
            order = sorted(
                (part for part in range(parts) if part != root),
                key=lambda part: -min((part - root) % parts, (root - part) % parts),
            )
            for part in order:
                pltpu.make_async_remote_copy(
                    src_ref=state_out.at[slot, part],
                    dst_ref=state.at[slot],
                    send_sem=s_send.at[slot],
                    recv_sem=s_recv.at[slot],
                    device_id={"gx": part},
                    device_id_type=MESH,
                ).start()
            state[slot] = state_out[slot, root]

        @pl.when(jnp.logical_not(here))
        def _():
            pltpu.make_async_copy(state.at[slot], state.at[slot], s_recv.at[slot]).wait()

    def finish(root, slot):
        here = gx == root

        @pl.when(here)
        def _():
            sent = state_out.at[slot, pl.ds(0, parts - 1)]
            pltpu.make_async_copy(sent, sent, s_send.at[slot]).wait()

        @pl.when(jnp.logical_not(here))
        def _():
            pltpu.make_async_copy(coef.at[slot], coef.at[slot], c_send.at[slot]).wait()

    to_next.wait_recv()
    to_prev.wait_recv()
    own = pltpu.roll(packed, 127, 1)
    other = jnp.where(even, edge_in[0], pltpu.roll(edge_in[1], 126, 1))
    own_q = pltpu.roll(own, 64, 1)
    other_q = pltpu.roll(other, 64, 1)
    outside = jnp.logical_or(
        jnp.logical_and(even, gy == 0),
        jnp.logical_and(jnp.logical_not(even), gy == rows - 1),
    )
    face = jnp.where(outside, 0.0, 0.3 / (own_q + other_q) * (other - own))
    rim = jnp.logical_or(lane == 0, lane == 127)
    for i in range(CELLS):
        extra = jnp.where(rim, pltpu.roll(face, (128 - 2 * i) % 128, 1), 0.0)
        r_ref[i] = h[i] * (r_ref[i] + extra)

    @pl.when(has_up)
    def _():
        to_down.wait_recv()

    @pl.when(is_last)
    def _():
        head_in[...] = jnp.ones_like(head_in)

    h_next = head_in[2]
    rho_start = face_weights(resistivity(head_in[0], head_in[1]), h_next)
    transfer(rho_start, 0)
    solve(first_root, 0)

    u, flux = state[0, 0], state[0, 1]
    u = u - rho_start * flux
    for i in range(CELLS):
        flux = flux + (r_ref[i] - h[i] * u)
        q_ref[i] = resistivity(0.5 * (f_ref[i] + u), k_ref[i])
        u = u - rho_ref[i] * flux
    rho_start = face_weights(resistivity(0.5 * (head_in[0] + u), head_in[1]), h_next)
    transfer(rho_start, 1)
    solve(second_root, 1)

    u, flux = state[1, 0], state[1, 1]
    u = u - rho_start * flux
    for i in range(CELLS):
        flux = flux + (r_ref[i] - h[i] * u)
        u_out[i] = u
        flux_out[i] = flux * (1.0 / CELLS)
        u = u - rho_ref[i] * flux

    to_next.wait_send()
    to_prev.wait_send()

    @pl.when(has_down)
    def _():
        to_down.wait_send()

    finish(first_root, 0)
    finish(second_root, 1)


def per_device(parts, rows, field_now, base_cond, spacing, source):
    whole = pl.BlockSpec(memory_space=pltpu.VMEM)
    tile = (8, 128)
    shape = jax.ShapeDtypeStruct(field_now.shape, jnp.float32)
    return pl.pallas_call(
        functools.partial(kernel, parts, rows),
        out_shape=[shape, shape],
        in_specs=[pl.BlockSpec(memory_space=pltpu.SMEM), whole, whole, whole],
        out_specs=[whole, whole],
        scratch_shapes=[
            pltpu.VMEM((CELLS, *tile), jnp.float32),
            pltpu.VMEM((CELLS, *tile), jnp.float32),
            pltpu.VMEM((CELLS, *tile), jnp.float32),
            pltpu.VMEM(tile, jnp.float32),
            pltpu.VMEM((2, *tile), jnp.float32),
            pltpu.VMEM((3, *tile), jnp.float32),
            pltpu.VMEM((3, *tile), jnp.float32),
            pltpu.VMEM((2, COEFS, *tile), jnp.float32),
            pltpu.VMEM((2, parts, COEFS, *tile), jnp.float32),
            pltpu.VMEM((2, parts, 2, *tile), jnp.float32),
            pltpu.VMEM((2, 2, *tile), jnp.float32),
            pltpu.SemaphoreType.DMA((2,)),
            pltpu.SemaphoreType.DMA((2,)),
            pltpu.SemaphoreType.DMA,
            pltpu.SemaphoreType.DMA,
            pltpu.SemaphoreType.DMA((2,)),
            pltpu.SemaphoreType.DMA((2,)),
            pltpu.SemaphoreType.DMA((2,)),
            pltpu.SemaphoreType.DMA((2,)),
        ],
        compiler_params=pltpu.CompilerParams(
            collective_id=0, has_side_effects=True, vmem_limit_bytes=16 * 1024 * 1024
        ),
    )(spacing, field_now, base_cond, source)


def solution(mesh):
    placed = (P("gx", None, "gy"), P("gx", None, "gy"), P("gx"), P("gx", None, "gy"))
    return jax.shard_map(
        functools.partial(per_device, mesh.shape["gx"], mesh.shape["gy"]),
        mesh=mesh,
        in_specs=placed,
        out_specs=(P("gx", None, "gy"), P("gx", None, "gy")),
        check_vma=False,
    )
```

```python
import functools

import jax
import jax.numpy as jnp
from jax import lax
from jax.experimental import pallas as pl
from jax.experimental.pallas import tpu as pltpu
from jax.sharding import PartitionSpec as P

MESH = pl.DeviceIdType.MESH
CELLS = 32
COEFS = 6
FIRST_ROOT = 5
SECOND_ROOT = 0


def resistivity(field, base_cond):
    square = field * field
    return (1.0 + square) / (base_cond * (1.0 + 2.0 * square))


def kernel(
    parts,
    rows,
    h_hbm,
    f_hbm,
    k_hbm,
    s_hbm,
    r_ref,
    rho_ref,
    width_ref,
    entry_ref,
    h_ref,
    f_ref,
    k_ref,
    s_ref,
    q_ref,
    edge,
    edge_in,
    head,
    head_in,
    coef,
    gather,
    state_out,
    state,
    load,
    y_send,
    y_recv,
    x_send,
    x_recv,
    c_send,
    c_recv,
    s_send,
    s_recv,
):
    gx = lax.axis_index("gx")
    gy = lax.axis_index("gy")
    first_root = FIRST_ROOT % parts
    second_root = SECOND_ROOT % parts
    roots = (first_root, second_root)
    has_up, has_down = gx < parts - 1, gx > 0
    has_next, has_prev = gy < rows - 1, gy > 0

    barrier = pltpu.get_barrier_semaphore()

    def greet(target):
        pl.semaphore_signal(barrier, inc=1, device_id=target, device_id_type=MESH)

    neighbours = (
        (has_next, {"gy": gy + 1}),
        (has_prev, {"gy": gy - 1}),
        (has_up, {"gx": gx + 1}),
        (has_down, {"gx": gx - 1}),
    )
    greetings = 0
    for there, target in neighbours:
        pl.when(there)(functools.partial(greet, target))
        greetings = greetings + there.astype(jnp.int32)

    loads = [
        pltpu.make_async_copy(source, target, load.at[i])
        for i, (source, target) in enumerate(
            ((f_hbm, f_ref), (k_hbm, k_ref), (s_hbm, s_ref), (h_hbm, h_ref))
        )
    ]
    for copy in loads:
        copy.start()

    def is_root(root):
        return gx == root

    for root in roots:
        greetings = greetings + 1 - is_root(root).astype(jnp.int32)

        @pl.when(is_root(root))
        def _():
            for step in range(1, parts):
                greet({"gx": lax.rem(gx + step, parts)})

    lane = lax.broadcasted_iota(jnp.int32, (8, 128), 1)
    plane = lax.broadcasted_iota(jnp.int32, (8, 128), 0)
    even = lane % 2 == 0
    pair = lane // 2

    loads[0].wait()
    loads[1].wait()

    packed = jnp.zeros((8, 128), jnp.float32)
    for i in range(CELLS):
        field = f_ref[i]
        q = resistivity(field, k_ref[i])
        q_ref[i] = q
        packed = jnp.where(pair == i, pltpu.roll(field, 2 * i + 1, 1), packed)
        packed = jnp.where(pair == i + 32, pltpu.roll(q, (64 + 2 * i + 1) % 128, 1), packed)
    edge[...] = packed
    loads[3].wait()
    spacing = h_ref[...]
    for i in range(CELLS):
        width_ref[i] = jnp.broadcast_to(spacing[:, i : i + 1], (8, 128))
    head[0] = f_ref[0]
    head[1] = k_ref[0]
    head[2] = width_ref[0]

    pl.semaphore_wait(barrier, greetings)

    def y_copy(slot, target):
        return pltpu.make_async_remote_copy(
            src_ref=edge,
            dst_ref=edge_in.at[slot],
            send_sem=y_send.at[slot],
            recv_sem=y_recv.at[slot],
            device_id={"gy": lax.rem(target + rows, rows)},
            device_id_type=MESH,
        )

    to_next, to_prev = y_copy(0, gy + 1), y_copy(1, gy - 1)
    pl.when(has_next)(to_next.start)
    pl.when(has_prev)(to_prev.start)
    to_down = pltpu.make_async_remote_copy(
        src_ref=head,
        dst_ref=head_in,
        send_sem=x_send,
        recv_sem=x_recv,
        device_id={"gx": lax.rem(gx + parts - 1, parts)},
        device_id_type=MESH,
    )

    @pl.when(has_down)
    def _():
        to_down.start()

    loads[2].wait()

    for i in range(CELLS):
        field, q = f_ref[i], q_ref[i]
        face_y = 0.3 / (q + pltpu.roll(q, 127, 1)) * (pltpu.roll(field, 127, 1) - field)
        face_y = jnp.where(lane == 127, 0.0, face_y)
        face_z = 0.2 / (q + pltpu.roll(q, 7, 0)) * (pltpu.roll(field, 7, 0) - field)
        face_z = jnp.where(plane == 7, 0.0, face_z)
        r_ref[i] = (
            field
            + (face_y - pltpu.roll(face_y, 1, 1))
            + (face_z - pltpu.roll(face_z, 1, 0))
            + s_ref[i]
        )

    h = [width_ref[i] for i in range(CELLS)]
    is_first = gx == 0
    is_last = gx == parts - 1

    def face_weights(q_next, h_next):
        scale = 1.0 / (16.0 * CELLS * CELLS)
        for i in range(CELLS - 1):
            rho_ref[i] = ((h[i] + h[i + 1]) * scale) * (q_ref[i] + q_ref[i + 1])
        q_last = q_ref[CELLS - 1]
        q_next = jnp.where(is_last, q_last, q_next)
        h_next = jnp.where(is_last, h[CELLS - 1], h_next)
        rho_ref[CELLS - 1] = ((h[CELLS - 1] + h_next) * scale) * (q_last + q_next)
        return jnp.where(is_first, (4.0 * h[0] * scale) * q_ref[0], 0.0)

    def transfer(rho_start, slot):
        one = jnp.ones((8, 128), jnp.float32)
        zero = jnp.zeros((8, 128), jnp.float32)
        u_a, f_a = one, zero
        u_b, f_b = zero - rho_start, one
        u_c, f_c = zero, zero
        for i in range(CELLS):
            rho = rho_ref[i]
            f_a = f_a - h[i] * u_a
            f_b = f_b - h[i] * u_b
            f_c = f_c + (r_ref[i] - h[i] * u_c)
            u_a = u_a - rho * f_a
            u_b = u_b - rho * f_b
            u_c = u_c - rho * f_c
        for c, value in enumerate((u_a, u_b, f_a, f_b, u_c, f_c)):
            coef[slot, c] = value

    def chain(slot):
        zero = jnp.zeros((8, 128), jnp.float32)
        w_u, w_f = zero, zero + 1.0
        p_u, p_f = zero, zero
        entries = []
        for part in range(parts):
            entries.append((w_u, w_f, p_u, p_f))
            m11, m12, m21, m22, b_u, b_f = (
                gather[slot * parts + part, c] for c in range(COEFS)
            )
            w_u, w_f = m11 * w_u + m12 * w_f, m21 * w_u + m22 * w_f
            p_u, p_f = m11 * p_u + m12 * p_f + b_u, m21 * p_u + m22 * p_f + b_f
        start = -p_u / w_u
        for part, (w_u, w_f, p_u, p_f) in enumerate(entries):
            state_out[slot * parts + part, 0] = w_u * start + p_u
            state_out[slot * parts + part, 1] = w_f * start + p_f

    def solve(root, slot):
        here = is_root(root)
        to_root = pltpu.make_async_remote_copy(
            src_ref=coef.at[slot],
            dst_ref=gather.at[slot * parts + gx],
            send_sem=c_send.at[slot],
            recv_sem=c_recv.at[slot],
            device_id={"gx": root},
            device_id_type=MESH,
        )
        pl.when(jnp.logical_not(here))(to_root.start)

        @pl.when(here)
        def _():
            gather[slot * parts + root] = coef[slot]
            arrived = gather.at[pl.ds(slot * parts, parts - 1)]
            pltpu.make_async_copy(arrived, arrived, c_recv.at[slot]).wait()
            chain(slot)
            order = sorted(
                (part for part in range(parts) if part != root),
                key=lambda part: min((part - root) % parts, (root - part) % parts),
                reverse=slot == 0,
            )
            for part in order:
                pltpu.make_async_remote_copy(
                    src_ref=state_out.at[slot * parts + part],
                    dst_ref=state.at[slot],
                    send_sem=s_send.at[slot],
                    recv_sem=s_recv.at[slot],
                    device_id={"gx": part},
                    device_id_type=MESH,
                ).start()
            state[slot] = state_out[slot * parts + root]

        @pl.when(jnp.logical_not(here))
        def _():
            pltpu.make_async_copy(state.at[slot], state.at[slot], s_recv.at[slot]).wait()

    def finish(root, slot):
        here = is_root(root)

        @pl.when(here)
        def _():
            sent = state_out.at[pl.ds(slot * parts, parts - 1)]
            pltpu.make_async_copy(sent, sent, s_send.at[slot]).wait()

        @pl.when(jnp.logical_not(here))
        def _():
            pltpu.make_async_copy(coef.at[slot], coef.at[slot], c_send.at[slot]).wait()

    pl.when(has_prev)(to_next.wait_recv)
    pl.when(has_next)(to_prev.wait_recv)

    @pl.when(jnp.logical_not(has_prev))
    def _():
        edge_in[0] = packed

    @pl.when(jnp.logical_not(has_next))
    def _():
        edge_in[1] = packed

    own = pltpu.roll(packed, 127, 1)
    other = jnp.where(even, edge_in[0], pltpu.roll(edge_in[1], 126, 1))
    own_q = pltpu.roll(own, 64, 1)
    other_q = pltpu.roll(other, 64, 1)
    outside = jnp.logical_or(
        jnp.logical_and(even, gy == 0),
        jnp.logical_and(jnp.logical_not(even), gy == rows - 1),
    )
    face = jnp.where(outside, 0.0, 0.3 / (own_q + other_q) * (other - own))
    rim = jnp.logical_or(lane == 0, lane == 127)
    for i in range(CELLS):
        extra = jnp.where(rim, pltpu.roll(face, (128 - 2 * i) % 128, 1), 0.0)
        r_ref[i] = h[i] * (r_ref[i] + extra)

    @pl.when(has_up)
    def _():
        to_down.wait_recv()

    @pl.when(is_last)
    def _():
        head_in[...] = jnp.ones_like(head_in)

    h_next = head_in[2]
    rho_start = face_weights(resistivity(head_in[0], head_in[1]), h_next)
    transfer(rho_start, 0)
    solve(first_root, 0)

    u, flux = state[0, 0], state[0, 1]
    u = u - rho_start * flux
    for i in range(CELLS):
        flux = flux + (r_ref[i] - h[i] * u)
        q_ref[i] = resistivity(0.5 * (f_ref[i] + u), k_ref[i])
        u = u - rho_ref[i] * flux
    rho_start = face_weights(resistivity(0.5 * (head_in[0] + u), head_in[1]), h_next)
    transfer(rho_start, 1)
    solve(second_root, 1)

    entry_ref[0] = state[1, 0] - rho_start * state[1, 1]
    entry_ref[1] = state[1, 1]
    pl.when(has_next)(to_next.wait_send)
    pl.when(has_prev)(to_prev.wait_send)

    @pl.when(has_down)
    def _():
        to_down.wait_send()

    finish(first_root, 0)
    finish(second_root, 1)


def sweep(r_ref, rho_ref, width_ref, entry_ref, u_out, flux_out):
    u, flux = entry_ref[0], entry_ref[1]
    for i in range(CELLS):
        flux = flux + (r_ref[i] - width_ref[i] * u)
        u_out[i] = u
        flux_out[i] = flux * (1.0 / CELLS)
        u = u - rho_ref[i] * flux


def per_device(parts, rows, field_now, base_cond, spacing, source):
    vmem = pl.BlockSpec(memory_space=pltpu.VMEM)
    tile = (8, 128)
    block = jax.ShapeDtypeStruct((CELLS, *tile), jnp.float32)
    parts_of_system = pl.pallas_call(
        functools.partial(kernel, parts, rows),
        out_shape=[pltpu.VMEM((n, *tile), jnp.float32) for n in (CELLS, CELLS, CELLS, 2)],
        in_specs=[pl.BlockSpec(memory_space=pltpu.HBM)] * 4,
        out_specs=[vmem] * 4,
        scratch_shapes=[
            pltpu.VMEM((1, CELLS), jnp.float32),
            pltpu.VMEM((CELLS, *tile), jnp.float32),
            pltpu.VMEM((CELLS, *tile), jnp.float32),
            pltpu.VMEM((CELLS, *tile), jnp.float32),
            pltpu.VMEM((CELLS, *tile), jnp.float32),
            pltpu.VMEM(tile, jnp.float32),
            pltpu.VMEM((2, *tile), jnp.float32),
            pltpu.VMEM((3, *tile), jnp.float32),
            pltpu.VMEM((3, *tile), jnp.float32),
            pltpu.VMEM((2, COEFS, *tile), jnp.float32),
            pltpu.VMEM((2 * parts, COEFS, *tile), jnp.float32),
            pltpu.VMEM((2 * parts, 2, *tile), jnp.float32),
            pltpu.VMEM((2, 2, *tile), jnp.float32),
            pltpu.SemaphoreType.DMA((4,)),
            pltpu.SemaphoreType.DMA((2,)),
            pltpu.SemaphoreType.DMA((2,)),
            pltpu.SemaphoreType.DMA,
            pltpu.SemaphoreType.DMA,
            pltpu.SemaphoreType.DMA((2,)),
            pltpu.SemaphoreType.DMA((2,)),
            pltpu.SemaphoreType.DMA((2,)),
            pltpu.SemaphoreType.DMA((2,)),
        ],
        compiler_params=pltpu.CompilerParams(
            collective_id=0, has_side_effects=True, vmem_limit_bytes=60 * 1024 * 1024
        ),
    )(spacing.reshape(1, CELLS), field_now, base_cond, source)
    return pl.pallas_call(
        sweep,
        out_shape=[block, block],
        in_specs=[vmem] * 4,
        out_specs=[vmem] * 2,
        compiler_params=pltpu.CompilerParams(vmem_limit_bytes=4 * 1024 * 1024),
    )(*parts_of_system)


def solution(mesh):
    placed = (P("gx", None, "gy"), P("gx", None, "gy"), P("gx"), P("gx", None, "gy"))
    return jax.shard_map(
        functools.partial(per_device, mesh.shape["gx"], mesh.shape["gy"]),
        mesh=mesh,
        in_specs=placed,
        out_specs=(P("gx", None, "gy"), P("gx", None, "gy")),
        check_vma=False,
    )
```

```python
import functools

import jax
import jax.numpy as jnp
from jax import lax
from jax.experimental import pallas as pl
from jax.experimental.pallas import tpu as pltpu
from jax.sharding import PartitionSpec as P

MESH = pl.DeviceIdType.MESH
CELLS = 32
COEFS = 6
FIRST_ROOT = 4
SECOND_ROOT = 0


def resistivity(field, base_cond):
    square = field * field
    return (1.0 + square) / (base_cond * (1.0 + 2.0 * square))


def kernel(
    parts,
    rows,
    h_hbm,
    f_hbm,
    k_hbm,
    s_hbm,
    r_ref,
    rho_ref,
    width_ref,
    entry_ref,
    h_ref,
    f_ref,
    k_ref,
    s_ref,
    q_ref,
    edge,
    edge_in,
    head,
    head_in,
    coef,
    gather,
    state_out,
    state,
    load,
    y_send,
    y_recv,
    x_send,
    x_recv,
    c_send,
    c_recv,
    s_send,
    s_recv,
):
    gx = lax.axis_index("gx")
    gy = lax.axis_index("gy")
    first_root = FIRST_ROOT % parts
    second_root = SECOND_ROOT % parts
    roots = (first_root, second_root)
    other_y = jnp.where(gy % 2 == 0, gy + 1, gy - 1)
    has_up, has_down = gx < parts - 1, gx > 0
    has_next, has_prev = gy < rows - 1, gy > 0

    barrier = pltpu.get_barrier_semaphore()

    def greet(target):
        pl.semaphore_signal(barrier, inc=1, device_id=target, device_id_type=MESH)

    neighbours = (
        (has_next, {"gy": gy + 1}),
        (has_prev, {"gy": gy - 1}),
        (has_up, {"gx": gx + 1}),
        (has_down, {"gx": gx - 1}),
    )
    greetings = 0
    for there, target in neighbours:
        pl.when(there)(functools.partial(greet, target))
        greetings = greetings + there.astype(jnp.int32)

    loads = [
        pltpu.make_async_copy(source, target, load.at[i])
        for i, (source, target) in enumerate(
            ((f_hbm, f_ref), (k_hbm, k_ref), (s_hbm, s_ref), (h_hbm, h_ref))
        )
    ]
    for copy in loads:
        copy.start()

    def is_root(root):
        return gx == root

    for root in roots:
        greetings = greetings + 1

        @pl.when(is_root(root))
        def _():
            for step in range(parts):
                greet({"gx": lax.rem(gx + step, parts), "gy": other_y})

    lane = lax.broadcasted_iota(jnp.int32, (8, 128), 1)
    plane = lax.broadcasted_iota(jnp.int32, (8, 128), 0)
    even = lane % 2 == 0
    pair = lane // 2

    loads[0].wait()
    loads[1].wait()

    packed = jnp.zeros((8, 128), jnp.float32)
    for i in range(CELLS):
        field = f_ref[i]
        q = resistivity(field, k_ref[i])
        q_ref[i] = q
        packed = jnp.where(pair == i, pltpu.roll(field, 2 * i + 1, 1), packed)
        packed = jnp.where(pair == i + 32, pltpu.roll(q, (64 + 2 * i + 1) % 128, 1), packed)
    edge[...] = packed
    loads[3].wait()
    spacing = h_ref[...]
    for i in range(CELLS):
        width_ref[i] = jnp.broadcast_to(spacing[:, i : i + 1], (8, 128))
    head[0] = f_ref[0]
    head[1] = k_ref[0]
    head[2] = width_ref[0]

    pl.semaphore_wait(barrier, greetings)

    def y_copy(slot, target):
        return pltpu.make_async_remote_copy(
            src_ref=edge,
            dst_ref=edge_in.at[slot],
            send_sem=y_send.at[slot],
            recv_sem=y_recv.at[slot],
            device_id={"gy": lax.rem(target + rows, rows)},
            device_id_type=MESH,
        )

    to_next, to_prev = y_copy(0, gy + 1), y_copy(1, gy - 1)
    pl.when(has_next)(to_next.start)
    pl.when(has_prev)(to_prev.start)
    to_down = pltpu.make_async_remote_copy(
        src_ref=head,
        dst_ref=head_in,
        send_sem=x_send,
        recv_sem=x_recv,
        device_id={"gx": lax.rem(gx + parts - 1, parts)},
        device_id_type=MESH,
    )

    @pl.when(has_down)
    def _():
        to_down.start()

    loads[2].wait()

    for i in range(CELLS):
        field, q = f_ref[i], q_ref[i]
        face_y = 0.3 / (q + pltpu.roll(q, 127, 1)) * (pltpu.roll(field, 127, 1) - field)
        face_y = jnp.where(lane == 127, 0.0, face_y)
        face_z = 0.2 / (q + pltpu.roll(q, 7, 0)) * (pltpu.roll(field, 7, 0) - field)
        face_z = jnp.where(plane == 7, 0.0, face_z)
        r_ref[i] = (
            field
            + (face_y - pltpu.roll(face_y, 1, 1))
            + (face_z - pltpu.roll(face_z, 1, 0))
            + s_ref[i]
        )

    h = [width_ref[i] for i in range(CELLS)]
    is_first = gx == 0
    is_last = gx == parts - 1

    def face_weights(q_next, h_next):
        scale = 1.0 / (16.0 * CELLS * CELLS)
        for i in range(CELLS - 1):
            rho_ref[i] = ((h[i] + h[i + 1]) * scale) * (q_ref[i] + q_ref[i + 1])
        q_last = q_ref[CELLS - 1]
        q_next = jnp.where(is_last, q_last, q_next)
        h_next = jnp.where(is_last, h[CELLS - 1], h_next)
        rho_ref[CELLS - 1] = ((h[CELLS - 1] + h_next) * scale) * (q_last + q_next)
        return jnp.where(is_first, (4.0 * h[0] * scale) * q_ref[0], 0.0)

    def transfer(rho_start, slot):
        one = jnp.ones((8, 128), jnp.float32)
        zero = jnp.zeros((8, 128), jnp.float32)
        u_a, f_a = one, zero
        u_b, f_b = zero - rho_start, one
        u_c, f_c = zero, zero
        for i in range(CELLS):
            rho = rho_ref[i]
            f_a = f_a - h[i] * u_a
            f_b = f_b - h[i] * u_b
            f_c = f_c + (r_ref[i] - h[i] * u_c)
            u_a = u_a - rho * f_a
            u_b = u_b - rho * f_b
            u_c = u_c - rho * f_c
        for c, value in enumerate((u_a, u_b, f_a, f_b, u_c, f_c)):
            coef[slot, c] = value

    def chain(slot):
        zero = jnp.zeros((8, 128), jnp.float32)
        w_u, w_f = zero, zero + 1.0
        p_u, p_f = zero, zero
        entries = []
        for part in range(parts):
            entries.append((w_u, w_f, p_u, p_f))
            m11, m12, m21, m22, b_u, b_f = (
                gather[slot * parts + part, c] for c in range(COEFS)
            )
            w_u, w_f = m11 * w_u + m12 * w_f, m21 * w_u + m22 * w_f
            p_u, p_f = m11 * p_u + m12 * p_f + b_u, m21 * p_u + m22 * p_f + b_f
        start = -p_u / w_u
        for part, (w_u, w_f, p_u, p_f) in enumerate(entries):
            state_out[slot * parts + part, 0] = w_u * start + p_u
            state_out[slot * parts + part, 1] = w_f * start + p_f

    def solve(root, slot):
        here = is_root(root)
        to_root = pltpu.make_async_remote_copy(
            src_ref=coef.at[slot],
            dst_ref=gather.at[slot * parts + gx],
            send_sem=c_send.at[slot],
            recv_sem=c_recv.at[slot],
            device_id={"gx": root, "gy": other_y},
            device_id_type=MESH,
        )
        to_root.start()

        @pl.when(here)
        def _():
            arrived = gather.at[pl.ds(slot * parts, parts)]
            pltpu.make_async_copy(arrived, arrived, c_recv.at[slot]).wait()
            chain(slot)
            order = sorted(
                range(parts),
                key=lambda part: min((part - root) % parts, (root - part) % parts),
                reverse=slot == 0,
            )
            for part in order:
                pltpu.make_async_remote_copy(
                    src_ref=state_out.at[slot * parts + part],
                    dst_ref=state.at[slot],
                    send_sem=s_send.at[slot],
                    recv_sem=s_recv.at[slot],
                    device_id={"gx": part, "gy": other_y},
                    device_id_type=MESH,
                ).start()

        pltpu.make_async_copy(state.at[slot], state.at[slot], s_recv.at[slot]).wait()

    def finish(root, slot):
        here = is_root(root)

        @pl.when(here)
        def _():
            sent = state_out.at[pl.ds(slot * parts, parts)]
            pltpu.make_async_copy(sent, sent, s_send.at[slot]).wait()

        @pl.when(gx >= 0)
        def _():
            pltpu.make_async_copy(coef.at[slot], coef.at[slot], c_send.at[slot]).wait()

    pl.when(has_prev)(to_next.wait_recv)
    pl.when(has_next)(to_prev.wait_recv)

    @pl.when(jnp.logical_not(has_prev))
    def _():
        edge_in[0] = packed

    @pl.when(jnp.logical_not(has_next))
    def _():
        edge_in[1] = packed

    own = pltpu.roll(packed, 127, 1)
    other = jnp.where(even, edge_in[0], pltpu.roll(edge_in[1], 126, 1))
    own_q = pltpu.roll(own, 64, 1)
    other_q = pltpu.roll(other, 64, 1)
    outside = jnp.logical_or(
        jnp.logical_and(even, gy == 0),
        jnp.logical_and(jnp.logical_not(even), gy == rows - 1),
    )
    face = jnp.where(outside, 0.0, 0.3 / (own_q + other_q) * (other - own))
    rim = jnp.logical_or(lane == 0, lane == 127)
    for i in range(CELLS):
        extra = jnp.where(rim, pltpu.roll(face, (128 - 2 * i) % 128, 1), 0.0)
        r_ref[i] = h[i] * (r_ref[i] + extra)

    @pl.when(has_up)
    def _():
        to_down.wait_recv()

    @pl.when(is_last)
    def _():
        head_in[...] = jnp.ones_like(head_in)

    h_next = head_in[2]
    rho_start = face_weights(resistivity(head_in[0], head_in[1]), h_next)
    transfer(rho_start, 0)
    solve(first_root, 0)

    u, flux = state[0, 0], state[0, 1]
    u = u - rho_start * flux
    for i in range(CELLS):
        flux = flux + (r_ref[i] - h[i] * u)
        q_ref[i] = resistivity(0.5 * (f_ref[i] + u), k_ref[i])
        u = u - rho_ref[i] * flux
    rho_start = face_weights(resistivity(0.5 * (head_in[0] + u), head_in[1]), h_next)
    transfer(rho_start, 1)
    solve(second_root, 1)

    entry_ref[0] = state[1, 0] - rho_start * state[1, 1]
    entry_ref[1] = state[1, 1]
    pl.when(has_next)(to_next.wait_send)
    pl.when(has_prev)(to_prev.wait_send)

    @pl.when(has_down)
    def _():
        to_down.wait_send()

    finish(first_root, 0)
    finish(second_root, 1)


def sweep(r_ref, rho_ref, width_ref, entry_ref, u_out, flux_out):
    u, flux = entry_ref[0], entry_ref[1]
    for i in range(CELLS):
        flux = flux + (r_ref[i] - width_ref[i] * u)
        u_out[i] = u
        flux_out[i] = flux * (1.0 / CELLS)
        u = u - rho_ref[i] * flux


def per_device(parts, rows, field_now, base_cond, spacing, source):
    vmem = pl.BlockSpec(memory_space=pltpu.VMEM)
    tile = (8, 128)
    block = jax.ShapeDtypeStruct((CELLS, *tile), jnp.float32)
    parts_of_system = pl.pallas_call(
        functools.partial(kernel, parts, rows),
        out_shape=[pltpu.VMEM((n, *tile), jnp.float32) for n in (CELLS, CELLS, CELLS, 2)],
        in_specs=[pl.BlockSpec(memory_space=pltpu.HBM)] * 4,
        out_specs=[vmem] * 4,
        scratch_shapes=[
            pltpu.VMEM((1, CELLS), jnp.float32),
            pltpu.VMEM((CELLS, *tile), jnp.float32),
            pltpu.VMEM((CELLS, *tile), jnp.float32),
            pltpu.VMEM((CELLS, *tile), jnp.float32),
            pltpu.VMEM((CELLS, *tile), jnp.float32),
            pltpu.VMEM(tile, jnp.float32),
            pltpu.VMEM((2, *tile), jnp.float32),
            pltpu.VMEM((3, *tile), jnp.float32),
            pltpu.VMEM((3, *tile), jnp.float32),
            pltpu.VMEM((2, COEFS, *tile), jnp.float32),
            pltpu.VMEM((2 * parts, COEFS, *tile), jnp.float32),
            pltpu.VMEM((2 * parts, 2, *tile), jnp.float32),
            pltpu.VMEM((2, 2, *tile), jnp.float32),
            pltpu.SemaphoreType.DMA((4,)),
            pltpu.SemaphoreType.DMA((2,)),
            pltpu.SemaphoreType.DMA((2,)),
            pltpu.SemaphoreType.DMA,
            pltpu.SemaphoreType.DMA,
            pltpu.SemaphoreType.DMA((2,)),
            pltpu.SemaphoreType.DMA((2,)),
            pltpu.SemaphoreType.DMA((2,)),
            pltpu.SemaphoreType.DMA((2,)),
        ],
        compiler_params=pltpu.CompilerParams(
            collective_id=0, has_side_effects=True, vmem_limit_bytes=60 * 1024 * 1024
        ),
    )(spacing.reshape(1, CELLS), field_now, base_cond, source)
    return pl.pallas_call(
        sweep,
        out_shape=[block, block],
        in_specs=[vmem] * 4,
        out_specs=[vmem] * 2,
        compiler_params=pltpu.CompilerParams(vmem_limit_bytes=4 * 1024 * 1024),
    )(*parts_of_system)


def solution(mesh):
    placed = (P("gx", None, "gy"), P("gx", None, "gy"), P("gx"), P("gx", None, "gy"))
    return jax.shard_map(
        functools.partial(per_device, mesh.shape["gx"], mesh.shape["gy"]),
        mesh=mesh,
        in_specs=placed,
        out_specs=(P("gx", None, "gy"), P("gx", None, "gy")),
        check_vma=False,
    )
```

```python
import functools

import jax
import jax.numpy as jnp
from jax import lax
from jax.experimental import pallas as pl
from jax.experimental.pallas import tpu as pltpu
from jax.sharding import PartitionSpec as P

MESH = pl.DeviceIdType.MESH
CELLS = 32
LAST = CELLS - 1
SCALE = 1.0 / (16.0 * CELLS * CELLS)
FIRST_ROOT = 4
SECOND_ROOT = 0


def resistivity(field, base_cond):
    square = field * field
    return (1.0 + square) / (base_cond * (1.0 + 2.0 * square))


def kernel(
    parts,
    rows,
    h_hbm,
    f_hbm,
    k_hbm,
    s_hbm,
    r_ref,
    rho_ref,
    width_ref,
    entry_ref,
    h_ref,
    f_ref,
    k_ref,
    s_ref,
    q_ref,
    edge,
    edge_in,
    head,
    head_in,
    matrix,
    vector,
    coef,
    matrices,
    vectors,
    coefs,
    corner_ref,
    answer,
    state,
    load,
    send,
    recv,
):
    gx = lax.axis_index("gx")
    gy = lax.axis_index("gy")
    first_root = FIRST_ROOT % parts
    second_root = SECOND_ROOT % parts
    is_even = gy % 2 == 0
    other_y = jnp.where(is_even, gy + 1, gy - 1)
    has_up, has_down = gx < parts - 1, gx > 0
    has_next, has_prev = gy < rows - 1, gy > 0
    first_here, second_here = gx == first_root, gx == second_root

    barrier = pltpu.get_barrier_semaphore()

    def greet(target):
        pl.semaphore_signal(barrier, inc=1, device_id=target, device_id_type=MESH)

    neighbours = (
        (has_next, {"gy": gy + 1}),
        (has_prev, {"gy": gy - 1}),
        (has_up, {"gx": gx + 1}),
        (has_down, {"gx": gx - 1}),
    )
    greetings = 2
    for there, target in neighbours:
        pl.when(there)(functools.partial(greet, target))
        greetings = greetings + there.astype(jnp.int32)

    loads = [
        pltpu.make_async_copy(source, target, load.at[i])
        for i, (source, target) in enumerate(
            ((f_hbm, f_ref), (k_hbm, k_ref), (s_hbm, s_ref), (h_hbm, h_ref))
        )
    ]
    for copy in loads:
        copy.start()

    for here in (first_here, second_here):

        @pl.when(here)
        def _():
            for step in range(parts):
                greet({"gx": lax.rem(gx + step, parts), "gy": other_y})

    lane = lax.broadcasted_iota(jnp.int32, (8, 128), 1)
    plane = lax.broadcasted_iota(jnp.int32, (8, 128), 0)
    even = lane % 2 == 0
    pair = lane // 2
    rim_pair = ((lane + 1) % 128) // 2
    rim = jnp.logical_or(lane == 0, lane == 127)

    loads[0].wait()
    loads[1].wait()

    packed = jnp.zeros((8, 128), jnp.float32)
    for i in range(CELLS):
        field = f_ref[i]
        q = resistivity(field, k_ref[i])
        q_ref[i] = q
        packed = jnp.where(pair == i, pltpu.roll(field, 2 * i + 1, 1), packed)
        packed = jnp.where(pair == i + 32, pltpu.roll(q, (64 + 2 * i + 1) % 128, 1), packed)
    loads[3].wait()
    spacing = h_ref[...]
    for i in range(CELLS):
        width_ref[i] = jnp.broadcast_to(spacing[:, i : i + 1], (8, 128))
    edge[...] = packed
    head[0] = f_ref[0]
    head[1] = k_ref[0]
    head[2] = width_ref[0]

    pl.semaphore_wait(barrier, greetings)

    def remote(index, source, target, **device):
        return pltpu.make_async_remote_copy(
            src_ref=source,
            dst_ref=target,
            send_sem=send.at[index],
            recv_sem=recv.at[index],
            device_id=device,
            device_id_type=MESH,
        )

    def wait_for(ref, semaphore):
        pltpu.make_async_copy(ref, ref, semaphore).wait()

    to_next = remote(0, edge, edge_in.at[0], gy=lax.rem(gy + 1, rows))
    to_prev = remote(1, edge, edge_in.at[1], gy=lax.rem(gy + rows - 1, rows))
    to_down = remote(2, head, head_in, gx=lax.rem(gx + parts - 1, parts))
    pl.when(has_next)(to_next.start)
    pl.when(has_prev)(to_prev.start)
    pl.when(has_down)(to_down.start)

    loads[2].wait()
    for i in range(CELLS):
        field, q = f_ref[i], q_ref[i]
        face_y = 0.3 / (q + pltpu.roll(q, 127, 1)) * (pltpu.roll(field, 127, 1) - field)
        face_y = jnp.where(lane == 127, 0.0, face_y)
        face_z = 0.2 / (q + pltpu.roll(q, 7, 0)) * (pltpu.roll(field, 7, 0) - field)
        face_z = jnp.where(plane == 7, 0.0, face_z)
        r_ref[i] = width_ref[i] * (
            field
            + (face_y - pltpu.roll(face_y, 1, 1))
            + (face_z - pltpu.roll(face_z, 1, 0))
            + s_ref[i]
        )

    def reduce_segment(weights):
        zero = jnp.zeros((8, 128), jnp.float32)
        packed_weights = zero
        s_u, s_f = zero + 1.0, zero
        p_u, p_f = zero, zero + 1.0
        b_u, b_f = zero, zero
        for i in reversed(range(CELLS)):
            h = width_ref[i]
            if i < LAST:
                rho = ((h + width_ref[i + 1]) * SCALE) * (q_ref[i] + q_ref[i + 1])
                rho_ref[i] = rho
                p_u = p_u - rho * s_u
                p_f = p_f - rho * s_f
            b_u = b_u + p_u * r_ref[i]
            b_f = b_f + p_f * r_ref[i]
            h_u, h_f = h * p_u, h * p_f
            s_u = s_u - h_u
            s_f = s_f - h_f
            if weights:
                packed_weights = jnp.where(
                    rim_pair == i, pltpu.roll(h_u, 2 * i, 1), packed_weights
                )
                packed_weights = jnp.where(
                    rim_pair == i + 32, pltpu.roll(h_f, 64 + 2 * i, 1), packed_weights
                )
        rho_start = jnp.where(gx == 0, (4.0 * SCALE) * width_ref[0] * q_ref[0], 0.0)
        p_u, p_f = p_u - rho_start * s_u, p_f - rho_start * s_f
        return rho_start, (s_u, p_u, s_f, p_f), (b_u, b_f), packed_weights

    def last_face(q_next):
        q_last, h_last = q_ref[LAST], width_ref[LAST]
        q_next = jnp.where(has_up, q_next, q_last)
        h_next = jnp.where(has_up, head_in[2], h_last)
        return ((h_last + h_next) * SCALE) * (q_last + q_next)

    def corner(m11, m12, m21):
        return (1.0 + m12 * m21) / m11

    def chain(slot, rows_of):
        zero = jnp.zeros((8, 128), jnp.float32)
        w_u, w_f = zero, zero + 1.0
        p_u, p_f = zero, zero
        entries = []
        for part in range(parts):
            entries.append((w_u, w_f, p_u, p_f))
            m11, m12, m21, m22, b_u, b_f, rho = rows_of(part)
            w_u, w_f = m11 * w_u + m12 * w_f, m21 * w_u + m22 * w_f
            p_u, p_f = m11 * p_u + m12 * p_f + b_u, m21 * p_u + m22 * p_f + b_f
            if rho is not None:
                w_u, p_u = w_u - rho * w_f, p_u - rho * p_f
        start = -p_u / w_u
        for part, (w_u, w_f, p_u, p_f) in enumerate(entries):
            answer[slot * parts + part, 0] = w_u * start + p_u
            answer[slot * parts + part, 1] = w_f * start + p_f

    def give_back(slot, index, root):
        order = sorted(
            range(parts),
            key=lambda part: min((part - root) % parts, (root - part) % parts),
            reverse=slot == 0,
        )
        for part in order:
            source = answer.at[slot * parts + part]
            remote(index, source, state.at[slot], gx=part, gy=other_y).start()

    rho_start, values, (b_u, b_f), packed_weights = reduce_segment(True)
    for c in range(3):
        matrix[c] = values[c]
    remote(3, matrix, matrices.at[gx], gx=first_root, gy=other_y).start()

    pl.when(has_prev)(to_next.wait_recv)
    pl.when(has_next)(to_prev.wait_recv)

    @pl.when(jnp.logical_not(has_prev))
    def _():
        edge_in[0] = packed

    @pl.when(jnp.logical_not(has_next))
    def _():
        edge_in[1] = packed

    own = pltpu.roll(packed, 127, 1)
    other = jnp.where(even, edge_in[0], pltpu.roll(edge_in[1], 126, 1))
    own_q = pltpu.roll(own, 64, 1)
    other_q = pltpu.roll(other, 64, 1)
    outside = jnp.logical_or(
        jnp.logical_and(even, gy == 0),
        jnp.logical_and(jnp.logical_not(even), gy == rows - 1),
    )
    faces = jnp.where(outside, 0.0, 0.3 / (own_q + other_q) * (other - own))
    faces = jnp.where(rim_pair < 32, faces, 0.0)
    total = (faces + pltpu.roll(faces, 64, 1)) * packed_weights
    for shift in (2, 4, 8, 16, 32):
        total = total + pltpu.roll(total, 128 - shift, 1)
    vector[0] = b_u + jnp.where(rim, total, 0.0)
    vector[1] = b_f + jnp.where(rim, pltpu.roll(total, 64, 1), 0.0)

    pl.when(has_up)(to_down.wait_recv)

    @pl.when(jnp.logical_not(has_up))
    def _():
        head_in[...] = jnp.ones_like(head_in)

    last_rho = last_face(resistivity(head_in[0], head_in[1]))
    vector[2] = last_rho
    remote(4, vector, vectors.at[gx], gx=first_root, gy=other_y).start()

    for i in range(CELLS):
        extra = jnp.where(rim, pltpu.roll(faces, (128 - 2 * i) % 128, 1), 0.0)
        r_ref[i] = r_ref[i] + width_ref[i] * extra

    @pl.when(first_here)
    def _():
        wait_for(matrices, recv.at[3])
        corners = [corner(*(matrices[part, c] for c in range(3))) for part in range(parts)]
        for part in range(parts):
            corner_ref[part] = corners[part]
        wait_for(vectors, recv.at[4])

        def rows_of(part):
            m = tuple(matrices[part, c] for c in range(3))
            return (*m, corner_ref[part], *(vectors[part, c] for c in range(3)))

        chain(0, rows_of)
        give_back(0, 5, first_root)

    wait_for(state.at[0], recv.at[5])

    u, flux = state[0, 0], state[0, 1]
    u = u - rho_start * flux
    for i in range(CELLS):
        flux = flux + (r_ref[i] - width_ref[i] * u)
        q_ref[i] = resistivity(0.5 * (f_ref[i] + u), k_ref[i])
        u = u - (rho_ref[i] if i < LAST else last_rho) * flux

    last_rho = last_face(resistivity(0.5 * (head_in[0] + u), head_in[1]))
    rho_start, (m11, m12, m21, m22), (b_u, b_f), _ = reduce_segment(False)
    values = (m11 - last_rho * m21, m12 - last_rho * m22, m21, b_u - last_rho * b_f, b_f)
    for c, value in enumerate(values):
        coef[c] = value
    remote(6, coef, coefs.at[gx], gx=second_root, gy=other_y).start()

    @pl.when(second_here)
    def _():
        wait_for(coefs, recv.at[6])

        def rows_of(part):
            m11, m12, m21, b_u, b_f = (coefs[part, c] for c in range(5))
            return m11, m12, m21, corner(m11, m12, m21), b_u, b_f, None

        chain(1, rows_of)
        give_back(1, 7, second_root)

    wait_for(state.at[1], recv.at[7])
    entry_ref[0] = state[1, 0] - rho_start * state[1, 1]
    entry_ref[1] = state[1, 1]

    pl.when(has_next)(to_next.wait_send)
    pl.when(has_prev)(to_prev.wait_send)
    pl.when(has_down)(to_down.wait_send)
    wait_for(matrix, send.at[3])
    wait_for(vector, send.at[4])
    wait_for(coef, send.at[6])

    @pl.when(first_here)
    def _():
        wait_for(answer.at[pl.ds(0, parts)], send.at[5])

    @pl.when(second_here)
    def _():
        wait_for(answer.at[pl.ds(parts, parts)], send.at[7])


def sweep(r_ref, rho_ref, width_ref, entry_ref, u_out, flux_out):
    u, flux = entry_ref[0], entry_ref[1]
    for i in range(CELLS):
        flux = flux + (r_ref[i] - width_ref[i] * u)
        u_out[i] = u
        flux_out[i] = flux * (1.0 / CELLS)
        if i < LAST:
            u = u - rho_ref[i] * flux


def per_device(parts, rows, field_now, base_cond, spacing, source):
    vmem = pl.BlockSpec(memory_space=pltpu.VMEM)
    block = jax.ShapeDtypeStruct((CELLS, 8, 128), jnp.float32)

    def tiles(*count):
        return pltpu.VMEM((*count, 8, 128), jnp.float32)

    system = pl.pallas_call(
        functools.partial(kernel, parts, rows),
        out_shape=[tiles(CELLS), tiles(CELLS), tiles(CELLS), tiles(2)],
        in_specs=[pl.BlockSpec(memory_space=pltpu.HBM)] * 4,
        out_specs=[vmem] * 4,
        scratch_shapes=[
            pltpu.VMEM((1, CELLS), jnp.float32),
            tiles(CELLS),
            tiles(CELLS),
            tiles(CELLS),
            tiles(CELLS),
            pltpu.VMEM((8, 128), jnp.float32),
            tiles(2),
            tiles(3),
            tiles(3),
            tiles(3),
            tiles(3),
            tiles(5),
            tiles(parts, 3),
            tiles(parts, 3),
            tiles(parts, 5),
            tiles(parts),
            tiles(2 * parts, 2),
            tiles(2, 2),
            pltpu.SemaphoreType.DMA((4,)),
            pltpu.SemaphoreType.DMA((8,)),
            pltpu.SemaphoreType.DMA((8,)),
        ],
        compiler_params=pltpu.CompilerParams(
            collective_id=0, has_side_effects=True, vmem_limit_bytes=60 * 1024 * 1024
        ),
    )(spacing.reshape(1, CELLS), field_now, base_cond, source)
    return pl.pallas_call(
        sweep,
        out_shape=[block, block],
        in_specs=[vmem] * 4,
        out_specs=[vmem] * 2,
        compiler_params=pltpu.CompilerParams(vmem_limit_bytes=4 * 1024 * 1024),
    )(*system)


def solution(mesh):
    placed = (P("gx", None, "gy"), P("gx", None, "gy"), P("gx"), P("gx", None, "gy"))
    return jax.shard_map(
        functools.partial(per_device, mesh.shape["gx"], mesh.shape["gy"]),
        mesh=mesh,
        in_specs=placed,
        out_specs=(P("gx", None, "gy"), P("gx", None, "gy")),
        check_vma=False,
    )
```

```python
import functools

import jax
import jax.numpy as jnp
from jax import lax
from jax.experimental import pallas as pl
from jax.experimental.pallas import tpu as pltpu
from jax.sharding import PartitionSpec as P

MESH = pl.DeviceIdType.MESH
CELLS = 32
LAST = CELLS - 1
SCALE = 1.0 / (16.0 * CELLS * CELLS)
FIRST_ROOT = 4
SECOND_ROOT = 0


def resistivity(field, base_cond):
    square = field * field
    return (1.0 + square) / (base_cond * (1.0 + 2.0 * square))


def kernel(
    parts,
    rows,
    h_hbm,
    f_hbm,
    k_hbm,
    s_hbm,
    modes_ref,
    entry_ref,
    r_ref,
    rho_ref,
    width_ref,
    h_ref,
    f_ref,
    k_ref,
    s_ref,
    q_ref,
    edge,
    edge_in,
    head,
    head_in,
    matrix,
    vector,
    coef,
    matrices,
    vectors,
    coefs,
    corner_ref,
    answer,
    state,
    load,
    send,
    recv,
):
    gx = lax.axis_index("gx")
    gy = lax.axis_index("gy")
    first_root = FIRST_ROOT % parts
    second_root = SECOND_ROOT % parts
    is_even = gy % 2 == 0
    other_y = jnp.where(is_even, gy + 1, gy - 1)
    has_up, has_down = gx < parts - 1, gx > 0
    has_next, has_prev = gy < rows - 1, gy > 0
    first_here, second_here = gx == first_root, gx == second_root

    barrier = pltpu.get_barrier_semaphore()

    def greet(target):
        pl.semaphore_signal(barrier, inc=1, device_id=target, device_id_type=MESH)

    neighbours = (
        (has_next, {"gy": gy + 1}),
        (has_prev, {"gy": gy - 1}),
        (has_up, {"gx": gx + 1}),
        (has_down, {"gx": gx - 1}),
    )
    greetings = 2
    for there, target in neighbours:
        pl.when(there)(functools.partial(greet, target))
        greetings = greetings + there.astype(jnp.int32)

    loads = [
        pltpu.make_async_copy(source, target, load.at[i])
        for i, (source, target) in enumerate(
            ((f_hbm, f_ref), (k_hbm, k_ref), (s_hbm, s_ref), (h_hbm, h_ref))
        )
    ]
    for copy in loads:
        copy.start()

    for here in (first_here, second_here):

        @pl.when(here)
        def _():
            for step in range(parts):
                greet({"gx": lax.rem(gx + step, parts), "gy": other_y})

    lane = lax.broadcasted_iota(jnp.int32, (8, 128), 1)
    plane = lax.broadcasted_iota(jnp.int32, (8, 128), 0)
    even = lane % 2 == 0
    pair = lane // 2
    rim_pair = ((lane + 1) % 128) // 2
    rim = jnp.logical_or(lane == 0, lane == 127)

    loads[0].wait()
    loads[1].wait()

    packed = jnp.zeros((8, 128), jnp.float32)
    for i in range(CELLS):
        field = f_ref[i]
        q = resistivity(field, k_ref[i])
        q_ref[i] = q
        packed = jnp.where(pair == i, pltpu.roll(field, 2 * i + 1, 1), packed)
        packed = jnp.where(pair == i + 32, pltpu.roll(q, (64 + 2 * i + 1) % 128, 1), packed)
    loads[3].wait()
    spacing = h_ref[...]
    for i in range(CELLS):
        width_ref[i] = jnp.broadcast_to(spacing[:, i : i + 1], (8, 128))
    edge[...] = packed
    head[0] = f_ref[0]
    head[1] = k_ref[0]
    head[2] = width_ref[0]

    pl.semaphore_wait(barrier, greetings)

    def remote(index, source, target, **device):
        return pltpu.make_async_remote_copy(
            src_ref=source,
            dst_ref=target,
            send_sem=send.at[index],
            recv_sem=recv.at[index],
            device_id=device,
            device_id_type=MESH,
        )

    def wait_for(ref, semaphore):
        pltpu.make_async_copy(ref, ref, semaphore).wait()

    to_next = remote(0, edge, edge_in.at[0], gy=lax.rem(gy + 1, rows))
    to_prev = remote(1, edge, edge_in.at[1], gy=lax.rem(gy + rows - 1, rows))
    to_down = remote(2, head, head_in, gx=lax.rem(gx + parts - 1, parts))
    pl.when(has_next)(to_next.start)
    pl.when(has_prev)(to_prev.start)
    pl.when(has_down)(to_down.start)

    loads[2].wait()
    for i in range(CELLS):
        field, q = f_ref[i], q_ref[i]
        face_y = 0.3 / (q + pltpu.roll(q, 127, 1)) * (pltpu.roll(field, 127, 1) - field)
        face_y = jnp.where(lane == 127, 0.0, face_y)
        face_z = 0.2 / (q + pltpu.roll(q, 7, 0)) * (pltpu.roll(field, 7, 0) - field)
        face_z = jnp.where(plane == 7, 0.0, face_z)
        r_ref[i] = width_ref[i] * (
            field
            + (face_y - pltpu.roll(face_y, 1, 1))
            + (face_z - pltpu.roll(face_z, 1, 0))
            + s_ref[i]
        )

    def reduce_segment(weights):
        zero = jnp.zeros((8, 128), jnp.float32)
        packed_weights = zero
        s_u, s_f = zero + 1.0, zero
        p_u, p_f = zero, zero + 1.0
        b_u, b_f = zero, zero
        for i in reversed(range(CELLS)):
            h = width_ref[i]
            if i < LAST:
                rho = ((h + width_ref[i + 1]) * SCALE) * (q_ref[i] + q_ref[i + 1])
                rho_ref[i] = rho
                p_u = p_u - rho * s_u
                p_f = p_f - rho * s_f
            b_u = b_u + p_u * r_ref[i]
            b_f = b_f + p_f * r_ref[i]
            h_u, h_f = h * p_u, h * p_f
            s_u = s_u - h_u
            s_f = s_f - h_f
            if weights:
                packed_weights = jnp.where(
                    rim_pair == i, pltpu.roll(h_u, 2 * i, 1), packed_weights
                )
                packed_weights = jnp.where(
                    rim_pair == i + 32, pltpu.roll(h_f, 64 + 2 * i, 1), packed_weights
                )
        rho_start = jnp.where(gx == 0, (4.0 * SCALE) * width_ref[0] * q_ref[0], 0.0)
        p_u, p_f = p_u - rho_start * s_u, p_f - rho_start * s_f
        return rho_start, (s_u, p_u, s_f, p_f), (b_u, b_f), packed_weights

    def propagate(rho_start, last_rho, keep):
        zero = jnp.zeros((8, 128), jnp.float32)
        u_a, f_a = zero + 1.0, zero
        u_b, f_b = zero - rho_start, zero + 1.0
        u_c, f_c = zero, zero
        for i in range(CELLS):
            h, rho = width_ref[i], rho_ref[i] if i < LAST else last_rho
            f_a = f_a - h * u_a
            f_b = f_b - h * u_b
            f_c = f_c + (r_ref[i] - h * u_c)
            for c, value in enumerate((u_a, u_b, u_c, f_a, f_b, f_c)):
                if c < 3 or keep:
                    modes_ref[i, c] = value
            u_a = u_a - rho * f_a
            u_b = u_b - rho * f_b
            u_c = u_c - rho * f_c
        return u_a, u_b, u_c

    def last_face(q_next):
        q_last, h_last = q_ref[LAST], width_ref[LAST]
        q_next = jnp.where(has_up, q_next, q_last)
        h_next = jnp.where(has_up, head_in[2], h_last)
        return ((h_last + h_next) * SCALE) * (q_last + q_next)

    def corner(m11, m12, m21):
        return (1.0 + m12 * m21) / m11

    def chain(slot, rows_of):
        zero = jnp.zeros((8, 128), jnp.float32)
        w_u, w_f = zero, zero + 1.0
        p_u, p_f = zero, zero
        entries = []
        for part in range(parts):
            entries.append((w_u, w_f, p_u, p_f))
            m11, m12, m21, m22, b_u, b_f, rho = rows_of(part)
            w_u, w_f = m11 * w_u + m12 * w_f, m21 * w_u + m22 * w_f
            p_u, p_f = m11 * p_u + m12 * p_f + b_u, m21 * p_u + m22 * p_f + b_f
            if rho is not None:
                w_u, p_u = w_u - rho * w_f, p_u - rho * p_f
        start = -p_u / w_u
        for part, (w_u, w_f, p_u, p_f) in enumerate(entries):
            answer[slot * parts + part, 0] = w_u * start + p_u
            answer[slot * parts + part, 1] = w_f * start + p_f

    def give_back(slot, index, root):
        order = sorted(
            range(parts),
            key=lambda part: min((part - root) % parts, (root - part) % parts),
            reverse=slot == 0,
        )
        for part in order:
            source = answer.at[slot * parts + part]
            remote(index, source, state.at[slot], gx=part, gy=other_y).start()

    rho_start, values, (b_u, b_f), packed_weights = reduce_segment(True)
    for c in range(3):
        matrix[c] = values[c]
    remote(3, matrix, matrices.at[gx], gx=first_root, gy=other_y).start()

    pl.when(has_prev)(to_next.wait_recv)
    pl.when(has_next)(to_prev.wait_recv)

    @pl.when(jnp.logical_not(has_prev))
    def _():
        edge_in[0] = packed

    @pl.when(jnp.logical_not(has_next))
    def _():
        edge_in[1] = packed

    own = pltpu.roll(packed, 127, 1)
    other = jnp.where(even, edge_in[0], pltpu.roll(edge_in[1], 126, 1))
    own_q = pltpu.roll(own, 64, 1)
    other_q = pltpu.roll(other, 64, 1)
    outside = jnp.logical_or(
        jnp.logical_and(even, gy == 0),
        jnp.logical_and(jnp.logical_not(even), gy == rows - 1),
    )
    faces = jnp.where(outside, 0.0, 0.3 / (own_q + other_q) * (other - own))
    faces = jnp.where(rim_pair < 32, faces, 0.0)
    total = (faces + pltpu.roll(faces, 64, 1)) * packed_weights
    for shift in (2, 4, 8, 16, 32):
        total = total + pltpu.roll(total, 128 - shift, 1)
    vector[0] = b_u + jnp.where(rim, total, 0.0)
    vector[1] = b_f + jnp.where(rim, pltpu.roll(total, 64, 1), 0.0)

    pl.when(has_up)(to_down.wait_recv)

    @pl.when(jnp.logical_not(has_up))
    def _():
        head_in[...] = jnp.ones_like(head_in)

    last_rho = last_face(resistivity(head_in[0], head_in[1]))
    vector[2] = last_rho
    remote(4, vector, vectors.at[gx], gx=first_root, gy=other_y).start()

    for i in range(CELLS):
        extra = jnp.where(rim, pltpu.roll(faces, (128 - 2 * i) % 128, 1), 0.0)
        r_ref[i] = r_ref[i] + width_ref[i] * extra

    @pl.when(first_here)
    def _():
        wait_for(matrices, recv.at[3])
        corners = [corner(*(matrices[part, c] for c in range(3))) for part in range(parts)]
        for part in range(parts):
            corner_ref[part] = corners[part]
        wait_for(vectors, recv.at[4])

        def rows_of(part):
            m = tuple(matrices[part, c] for c in range(3))
            return (*m, corner_ref[part], *(vectors[part, c] for c in range(3)))

        chain(0, rows_of)
        give_back(0, 5, first_root)

    u_a, u_b, u_c = propagate(rho_start, last_rho, False)
    wait_for(state.at[0], recv.at[5])

    u_in, f_in = state[0, 0], state[0, 1]
    for i in range(CELLS):
        u = modes_ref[i, 0] * u_in + modes_ref[i, 1] * f_in + modes_ref[i, 2]
        q_ref[i] = resistivity(0.5 * (f_ref[i] + u), k_ref[i])
    u = u_a * u_in + u_b * f_in + u_c

    last_rho = last_face(resistivity(0.5 * (head_in[0] + u), head_in[1]))
    rho_start, (m11, m12, m21, m22), (b_u, b_f), _ = reduce_segment(False)
    values = (m11 - last_rho * m21, m12 - last_rho * m22, m21, b_u - last_rho * b_f, b_f)
    for c, value in enumerate(values):
        coef[c] = value
    remote(6, coef, coefs.at[gx], gx=second_root, gy=other_y).start()

    @pl.when(second_here)
    def _():
        wait_for(coefs, recv.at[6])

        def rows_of(part):
            m11, m12, m21, b_u, b_f = (coefs[part, c] for c in range(5))
            return m11, m12, m21, corner(m11, m12, m21), b_u, b_f, None

        chain(1, rows_of)
        give_back(1, 7, second_root)

    propagate(rho_start, last_rho, True)
    wait_for(state.at[1], recv.at[7])
    entry_ref[...] = state[1]

    pl.when(has_next)(to_next.wait_send)
    pl.when(has_prev)(to_prev.wait_send)
    pl.when(has_down)(to_down.wait_send)
    wait_for(matrix, send.at[3])
    wait_for(vector, send.at[4])
    wait_for(coef, send.at[6])

    @pl.when(first_here)
    def _():
        wait_for(answer.at[pl.ds(0, parts)], send.at[5])

    @pl.when(second_here)
    def _():
        wait_for(answer.at[pl.ds(parts, parts)], send.at[7])


def combine(modes_ref, entry_ref, u_out, flux_out):
    u, flux = entry_ref[0], entry_ref[1]
    for i in range(CELLS):
        u_a, u_b, u_c, f_a, f_b, f_c = (modes_ref[i, c] for c in range(6))
        u_out[i] = u_a * u + u_b * flux + u_c
        flux_out[i] = (f_a * u + f_b * flux + f_c) * (1.0 / CELLS)


def per_device(parts, rows, field_now, base_cond, spacing, source):
    vmem = pl.BlockSpec(memory_space=pltpu.VMEM)
    block = jax.ShapeDtypeStruct((CELLS, 8, 128), jnp.float32)

    def tiles(*count):
        return pltpu.VMEM((*count, 8, 128), jnp.float32)

    system = pl.pallas_call(
        functools.partial(kernel, parts, rows),
        out_shape=[tiles(CELLS, 6), tiles(2)],
        in_specs=[pl.BlockSpec(memory_space=pltpu.HBM)] * 4,
        out_specs=[vmem] * 2,
        scratch_shapes=[
            tiles(CELLS),
            tiles(CELLS),
            tiles(CELLS),
            pltpu.VMEM((1, CELLS), jnp.float32),
            tiles(CELLS),
            tiles(CELLS),
            tiles(CELLS),
            tiles(CELLS),
            pltpu.VMEM((8, 128), jnp.float32),
            tiles(2),
            tiles(3),
            tiles(3),
            tiles(3),
            tiles(3),
            tiles(5),
            tiles(parts, 3),
            tiles(parts, 3),
            tiles(parts, 5),
            tiles(parts),
            tiles(2 * parts, 2),
            tiles(2, 2),
            pltpu.SemaphoreType.DMA((4,)),
            pltpu.SemaphoreType.DMA((8,)),
            pltpu.SemaphoreType.DMA((8,)),
        ],
        compiler_params=pltpu.CompilerParams(
            collective_id=0, has_side_effects=True, vmem_limit_bytes=60 * 1024 * 1024
        ),
    )(spacing.reshape(1, CELLS), field_now, base_cond, source)
    return pl.pallas_call(
        combine,
        out_shape=[block, block],
        in_specs=[vmem] * 2,
        out_specs=[vmem] * 2,
        compiler_params=pltpu.CompilerParams(vmem_limit_bytes=4 * 1024 * 1024),
    )(*system)


def solution(mesh):
    placed = (P("gx", None, "gy"), P("gx", None, "gy"), P("gx"), P("gx", None, "gy"))
    return jax.shard_map(
        functools.partial(per_device, mesh.shape["gx"], mesh.shape["gy"]),
        mesh=mesh,
        in_specs=placed,
        out_specs=(P("gx", None, "gy"), P("gx", None, "gy")),
        check_vma=False,
    )
```
